32 devices in a mesh: domain: 16 (over z, y, core), band: 2 (over x).
Axes of the slice: x: 2, y: 2, z: 4, core: 2. Of those that a mesh axis runs over, the one named last changes fastest.
Arguments:
- orbitals: float32 [8, 96, 36864], P('band', 'domain'), may hold values from -6 to 6
- potential: float32 [96, 36864], P('domain'), may hold values from -1.5 to 1.5
- coefficients: float32 [8, 8], replicated, may hold values from -2 to 2
- owners: int32 [1], replicated, may hold values from 0 to 7
Outputs:
- filtered: float32 [8, 96, 36864], P('band', 'domain')
- rotated: float32 [8, 96, 36864], P('band', 'domain')
The draws below stay inside these ranges and needn't reach their ends.
All inputs are finite; a program needn't handle non-finite values.
Results may differ from the reference program's by a relative error of at most 0.0001.
Values sent between devices are 32-bit elements; how exact they have to be, the bound alone decides.
A program may use at most 256 MiB of HBM per device.

```python
import jax
import jax.numpy as jnp
from jax import lax

B_DEV = 4
NZ = 192
PLANE = 36864
DEG = 3
ROUNDS = 1
NX = 96
NB = 8
N_BAND = 2


def shard_levels(rng, extent, shards, smallest, top_value):
    level, own = 1.0, jax.random.fold_in(rng, 6)
    for axis_at, blocks in shards:
        draws = jnp.exp(jax.random.uniform(jax.random.fold_in(own, axis_at), (blocks,), jnp.float32, smallest / len(shards), top_value / len(shards)))
        level = level * jnp.repeat(draws, extent[axis_at] // blocks).reshape([-1 if axis == axis_at else 1 for axis in range(len(extent))])
    return level


def bell_draw(own_key, dims, spread, reach, cuts=(), kind=jnp.bfloat16):
    loudness = shard_levels(own_key, dims, cuts, -0.22, 0.18) if cuts else 1.0
    drawn = jax.random.normal(own_key, dims, jnp.float32) * spread * loudness
    return jnp.minimum(jnp.maximum(drawn, -reach), reach).astype(kind)


def setup_inputs(seed: int = 0) -> dict:
    key_of = jax.random.split(jax.random.key(seed), 5)
    return {
        "orbitals": bell_draw(key_of[0], (NB, NX, PLANE), 1.0, 6.0, ((0, 2), (1, 16)), jnp.float32),
        "potential": jnp.clip(jax.random.uniform(key_of[1], (NX, PLANE), jnp.float32, -1.5, 1.5) * shard_levels(key_of[1], (NX, PLANE), ((0, 16),), -0.4, 0.0), -1.5, 1.5),
        "coefficients": bell_draw(key_of[2], (NB, NB), (B_DEV * (1 + ROUNDS)) ** -0.5, 2.0, (), jnp.float32),
        "owners": jax.random.randint(key_of[3], (ROUNDS,), 0, NB).astype(jnp.int32),
    }


lap_coeffs = (-205.0 / 72.0, 8.0 / 5.0, -1.0 / 5.0, 8.0 / 315.0, -1.0 / 560.0)


def hamiltonian(field, potential):
    cells_x = field.shape[1]
    plane = field.shape[2]
    column_z = jnp.arange(plane).astype(jnp.int32) % NZ
    padded_x = jnp.pad(field, ((0, 0), (4, 4), (0, 0)), mode="wrap")
    padded_y = jnp.pad(field, ((0, 0), (0, 0), (4 * NZ, 4 * NZ)))
    padded_z = jnp.pad(field, ((0, 0), (0, 0), (4, 4)))
    summed = 3.0 * lap_coeffs[0] * field
    for shift in range(1, 5):
        weight_k = lap_coeffs[shift]
        upper_ok = (column_z + shift < NZ).astype(field.dtype)
        lower_ok = (column_z - shift >= 0).astype(field.dtype)
        summed = summed + weight_k * (padded_x[:, 4 + shift:4 + shift + cells_x] + padded_x[:, 4 - shift:4 - shift + cells_x])
        summed = summed + weight_k * (padded_y[:, :, (4 + shift) * NZ:(4 + shift) * NZ + plane] + padded_y[:, :, (4 - shift) * NZ:(4 - shift) * NZ + plane])
        summed = summed + weight_k * (padded_z[:, :, 4 + shift:4 + shift + plane] * upper_ok + padded_z[:, :, 4 - shift:4 - shift + plane] * lower_ok)
    return -0.5 * summed + potential[None] * field


def chebyshev(block, potential):
    previous = block
    current = (hamiltonian(block, potential) - 6.0 * block) / 5.0
    for level in range(DEG - 1):
        following = 2.0 * (hamiltonian(current, potential) - 6.0 * current) / 5.0 - previous
        previous = current
        current = following
    return current


def reference(orbitals, potential, coefficients, owners):
    blocks = orbitals.reshape(N_BAND, B_DEV, NX, PLANE)

    def filter_block(single_block):
        return chebyshev(single_block, potential)

    filtered = lax.map(filter_block, blocks)
    coeff_blocks = coefficients.reshape(N_BAND, B_DEV, N_BAND, B_DEV)

    def rotate_block(index):
        summed = jnp.einsum("bxp,bc->cxp", filtered[index], coeff_blocks[index, :, index, :], precision=lax.Precision.HIGHEST)
        for turn in range(ROUNDS):
            source = owners[turn] // B_DEV
            offset = owners[turn] % B_DEV
            rolled = jnp.roll(filtered[source], -offset, axis=0)
            summed = summed + jnp.einsum("bxp,bc->cxp", rolled, coeff_blocks[source, :, index, :], precision=lax.Precision.HIGHEST)
        return summed

    rotated = lax.map(rotate_block, jnp.arange(N_BAND).astype(jnp.int32))
    return filtered.reshape(NB, NX, PLANE), rotated.reshape(NB, NX, PLANE)
```

```python
import functools

import jax
import jax.numpy as jnp
from jax import lax
from jax.experimental import pallas as pl
from jax.experimental.pallas import tpu as pltpu
from jax.sharding import PartitionSpec as P

LANES = 128
HALO = 4
PAD = 8
MESH = pl.DeviceIdType.MESH

lap_coeffs = (-205.0 / 72.0, 8.0 / 5.0, -1.0 / 5.0, 8.0 / 315.0, -1.0 / 560.0)
CENTER = 6.0
HALF = 5.0


def stencil_planes(out_store, v, prev, pot, rows, stride, first, count):
    weights = [-0.5 * c / HALF for c in lap_coeffs]
    blocks = rows // 24
    lane = lax.broadcasted_iota(jnp.int32, (8, LANES), 1)
    high = lane >= 64
    zero = jnp.zeros((8, LANES), jnp.float32)

    def block(index, carry):
        plane = first + index // blocks
        row = (index % blocks) * 24
        base = PAD + (plane + HALO) * stride + row

        def at(ref, start):
            return ref[pl.ds(start, 8, stride=3), :]

        near = {t: at(v, base + t) for t in range(-6, 9)}
        for t in range(3):
            x = near[t]
            nxt = near[t + 1] if t < 2 else zero
            prv = near[t - 1] if t > 0 else zero
            total = at(pot, plane * rows + row + t) * x
            odd = None
            for k in range(1, 5):
                up, down = lane < k, lane >= LANES - k
                if t == 1:
                    fill_up = jnp.where(high, 0.0, nxt)
                    fill_down = jnp.where(high, prv, 0.0)
                    up = up | (high & (lane < 64 + k))
                    down = down | ((lane >= 64 - k) & (lane < 64))
                else:
                    fill_up, fill_down = nxt, prv
                plus = pltpu.roll(jnp.where(up, fill_up, x), LANES - k, 1)
                minus = pltpu.roll(jnp.where(down, fill_down, x), k, 1)
                pairs = plus + minus
                pairs = pairs + (at(v, base + t + k * stride) + at(v, base + t - k * stride))
                if k % 2 == 0:
                    jump = 3 * k // 2
                    pairs = pairs + (near[t + jump] + near[t - jump])
                else:
                    low_jump = (3 * k) // 2
                    half = jnp.where(
                        high,
                        near[t + low_jump] + near[t - low_jump - 1],
                        near[t + low_jump + 1] + near[t - low_jump],
                    )
                    half = weights[k] * half
                    odd = half if odd is None else odd + half
                total = total + weights[k] * pairs
            total = total + pltpu.roll(odd, 64, 1)
            if prev is not None:
                total = (total + total) - at(prev, base + t)
            out_store(plane, row + t, total)
        return carry

    lax.fori_loop(0, count * blocks, block, 0)


def filter_kernel(
    layers, bands, planes, rows, stride, orbitals, potential, mix, *refs
):
    group = 4
    own = group * planes
    if bands == 2:
        out_f, out_r = refs[:2]
        refs = refs[2:]
    else:
        out_f, out_r = refs[0], None
        refs = refs[1:]
    (v0, v1, v2, v3, pot, stage, pot_stage, recv, local_sem, in_send, in_recv,
     pot_send, pot_recv, halo_send, halo_recv, out_send, out_recv) = refs
    me = lax.axis_index("domain")
    band = lax.axis_index("band")
    g = lax.rem(me, group)
    layer = me // group
    root = layer * group
    left = lax.rem(layer + layers - 1, layers) * group + g
    right = lax.rem(layer + 1, layers) * group + g
    core = root + (g + 1 - 2 * lax.rem(g, 2))
    across = root + lax.rem(g + 2, group)
    g_across = lax.rem(g + 2, group)

    barrier = pltpu.get_barrier_semaphore()
    friends = [(root + lax.rem(g + d, group), band) for d in range(1, group)] + [(left, band), (right, band)]
    if bands == 2:
        friends += [(root + d, 1 - band) for d in range(group)]
    for friend in friends:
        pl.semaphore_signal(barrier, inc=1, device_id=friend, device_id_type=MESH)
    mine_orbital = pltpu.make_async_copy(orbitals.at[g], stage.at[g], local_sem.at[0])
    mine_orbital.start()
    mine_pot = pltpu.make_async_copy(potential, pot_stage.at[g], local_sem.at[1])
    mine_pot.start()
    pl.semaphore_wait(barrier, len(friends))

    def orbital_send(d):
        q = lax.rem(g + d, group)
        return pltpu.make_async_remote_copy(
            orbitals.at[q], stage.at[g], in_send.at[d - 1], in_recv.at[d - 1],
            device_id=(root + q, band), device_id_type=MESH)

    def orbital_arrival(d):
        slot = stage.at[lax.rem(g + group - d, group)]
        pltpu.make_async_copy(slot, slot, in_recv.at[d - 1]).wait()

    for d in (2, 1, 3):
        orbital_send(d).start()

    gap = jnp.zeros((PAD, LANES), jnp.float32)

    def clear(index, carry):
        at = pl.multiple_of((index + HALO) * stride, 8)
        for ref in (v0, v1, v2):
            ref[pl.ds(at, PAD), :] = gap
        return carry

    lax.fori_loop(0, own + 1, clear, 0)

    def spread_planes(source, slot, store):
        def step(tile, carry):
            columns = pl.ds(pl.multiple_of(tile * LANES, LANES), LANES)
            store(tile, source[slot, :, columns])
            return carry

        lax.fori_loop(0, rows, step, 0, unroll=8)

    def unpack_orbital(slot):
        def store(tile, value):
            v0[pl.ds(PAD + (HALO + slot * planes) * stride + tile, planes, stride=stride), :] = value

        spread_planes(stage, slot, store)

    def unpack_pot(slot):
        def store(tile, value):
            scaled = (value - (CENTER + 1.5 * lap_coeffs[0])) * (1.0 / HALF)
            pot[pl.ds(slot * planes * rows + tile, planes, stride=rows), :] = scaled

        spread_planes(pot_stage, slot, store)

    mine_orbital.wait()
    unpack_orbital(g)
    for d in (1, 3, 2):
        orbital_arrival(d)
        unpack_orbital(lax.rem(g + group - d, group))

    length = HALO * stride - PAD
    spots = (PAD, PAD + HALO * stride, PAD + own * stride, PAD + (own + HALO) * stride)

    def halo_copies(level):
        ref = (v0, v1, v2)[level]
        low, first, last, high = (ref.at[pl.ds(s, length), :] for s in spots)
        return (
            pltpu.make_async_remote_copy(
                first, high, halo_send.at[level, 0], halo_recv.at[level, 0],
                device_id=(left, band), device_id_type=MESH),
            pltpu.make_async_remote_copy(
                last, low, halo_send.at[level, 1], halo_recv.at[level, 1],
                device_id=(right, band), device_id_type=MESH),
        )

    def start_halo(level):
        for copy in halo_copies(level):
            copy.start()

    def wait_halo(level):
        for copy in halo_copies(level):
            copy.wait_recv()

    start_halo(0)

    pot_core = pltpu.make_async_remote_copy(
        potential, pot_stage.at[g], pot_send.at[0], pot_recv.at[0], device_id=(core, band), device_id_type=MESH)
    pot_across = pltpu.make_async_remote_copy(
        potential, pot_stage.at[g], pot_send.at[1], pot_recv.at[1], device_id=(across, band), device_id_type=MESH)
    pot_relay = pltpu.make_async_remote_copy(
        pot_stage.at[g_across], pot_stage.at[g_across], pot_send.at[2], pot_recv.at[2],
        device_id=(core, band), device_id_type=MESH)
    pot_across.start()
    pot_core.start()
    g_core = g + 1 - 2 * lax.rem(g, 2)
    mine_pot.wait()
    unpack_pot(g)
    pot_core.wait_recv()
    unpack_pot(g_core)
    pot_across.wait_recv()
    pot_relay.start()
    unpack_pot(g_across)
    pot_relay.wait_recv()
    unpack_pot(lax.rem(g_core + 2, group))

    def padded(ref):
        def store(plane, row, value):
            ref[pl.ds(PAD + (plane + HALO) * stride + row, 8, stride=3), :] = value
        return store

    def plain(plane, row, value):
        v3[pl.ds(plane * rows + row, 8, stride=3), :] = value

    def level(number, first, count):
        if number == 1:
            stencil_planes(padded(v1), v0, None, pot, rows, stride, first, count)
        elif number == 2:
            stencil_planes(padded(v2), v1, v0, pot, rows, stride, first, count)
        else:
            stencil_planes(plain, v2, v1, pot, rows, stride, first, count)

    def piece_span(home, piece):
        start = 2 * (home % 2) if piece == 0 else 4 * (1 - home % 2)
        return start * rows, (4 if piece == 0 else 2) * rows

    def out_copies(home, piece):
        start, size = piece_span(home, piece)
        source = v3.at[pl.ds(home * planes * rows + start, size), :]
        remote = pltpu.make_async_remote_copy(
            source, recv.at[g, pl.ds(start, size), :], out_send.at[0, home, piece], out_recv.at[0, g, piece],
            device_id=(root + home, band), device_id_type=MESH)
        local = pltpu.make_async_copy(
            source, recv.at[g, pl.ds(start, size), :], out_recv.at[0, g, piece])
        peer = None
        if bands == 2:
            peer = pltpu.make_async_remote_copy(
                source, recv.at[group + g, pl.ds(start, size), :], out_send.at[1, home, piece],
                out_recv.at[1, g, piece], device_id=(root + home, 1 - band), device_id_type=MESH)
        return remote, local, peer

    def start_out(home, piece):
        remote, local, peer = out_copies(home, piece)
        if peer is not None:
            peer.start()

        @pl.when(g != home)
        def _():
            remote.start()

        @pl.when(g == home)
        def _():
            local.start()

    level(1, 4, own - 8)
    wait_halo(0)
    level(1, 0, 4)
    level(1, own - 4, 4)
    start_halo(1)
    level(2, 4, own - 8)
    level(3, 8, own - 16)
    start_out(1, 0)
    start_out(2, 0)
    wait_halo(1)
    level(2, 0, 4)
    level(2, own - 4, 4)
    start_halo(2)
    level(3, 4, 4)
    level(3, own - 8, 4)
    for home in range(group):
        start_out(home, 1)
    wait_halo(2)
    level(3, 0, 4)
    level(3, own - 4, 4)
    start_out(0, 0)
    start_out(3, 0)

    mine_start4 = 2 * lax.rem(g, 2) * rows
    mine_start2 = 4 * (1 - lax.rem(g, 2)) * rows
    for peer in range(bands if bands == 2 else 1):
        for q in range(group):
            for piece, start, size in ((0, mine_start4, 4 * rows), (1, mine_start2, 2 * rows)):
                where = recv.at[peer * group + q, pl.ds(pl.multiple_of(start, 8), size), :]
                pltpu.make_async_copy(where, where, out_recv.at[peer, q, piece]).wait()

    def finish(tile, carry):
        columns = pl.ds(pl.multiple_of(tile * LANES, LANES), LANES)
        inputs = [recv[i, pl.ds(tile, planes, stride=rows), :] for i in range(group * (2 if bands == 2 else 1))]
        for i in range(group):
            out_f[i, :, columns] = inputs[i]
        if out_r is not None:
            for c in range(group):
                total = mix[0, c] * inputs[0]
                for i in range(1, 2 * group):
                    total = total + mix[i, c] * inputs[i]
                out_r[c, :, columns] = total
        return carry

    lax.fori_loop(0, rows, finish, 0, unroll=2)

    for d in range(1, group):
        orbital_send(d).wait_send()
    for copy in (pot_core, pot_across, pot_relay):
        copy.wait_send()
    for number in range(3):
        for copy in halo_copies(number):
            copy.wait_send()
    for home in range(group):
        for piece in range(2):
            remote, local, peer = out_copies(home, piece)
            if peer is not None:
                peer.wait_send()

            @pl.when(g != home)
            def _():
                remote.wait_send()


def run_filter(orbitals, potential, mix, layers, bands):
    width, planes, cells = orbitals.shape
    rows = cells // LANES
    stride = rows + PAD
    own = width * planes
    padded_rows = (own + 2 * HALO) * stride + PAD
    f32 = jnp.float32
    count = 2 if bands == 2 else 1
    dma = pltpu.SemaphoreType.DMA
    shape = jax.ShapeDtypeStruct(orbitals.shape, f32)
    any_spec = pl.BlockSpec(memory_space=pl.ANY)
    return pl.pallas_call(
        functools.partial(filter_kernel, layers, bands, planes, rows, stride),
        out_shape=[shape] * count,
        in_specs=[any_spec, any_spec, pl.BlockSpec(memory_space=pltpu.SMEM)],
        out_specs=[pl.BlockSpec(memory_space=pltpu.VMEM)] * count,
        scratch_shapes=[
            pltpu.VMEM((padded_rows, LANES), f32),
            pltpu.VMEM((padded_rows, LANES), f32),
            pltpu.VMEM((padded_rows, LANES), f32),
            pltpu.VMEM((own * rows, LANES), f32),
            pltpu.VMEM((own * rows, LANES), f32),
            pltpu.VMEM((width, planes, cells), f32),
            pltpu.VMEM((width, planes, cells), f32),
            pltpu.VMEM((count * width, planes * rows, LANES), f32),
            dma((2,)), dma((3,)), dma((3,)), dma((3,)), dma((3,)),
            dma((3, 2)), dma((3, 2)), dma((2, 4, 2)), dma((2, 4, 2)),
        ],
        compiler_params=pltpu.CompilerParams(
            collective_id=0, has_side_effects=True, vmem_limit_bytes=60 * 1024 * 1024
        ),
    )(orbitals, potential, mix)


def spread(value, axis, source):
    kept = jnp.where(lax.axis_index(axis) == source, value, 0).astype(value.dtype)
    return lax.psum(kept, axis)


def mixing(block, coefficients, source, target, width):
    part_coeffs = lax.dynamic_slice(coefficients, (source * width, target * width), (width, width))
    return jnp.einsum("bxp,bc->cxp", block, part_coeffs, precision=lax.Precision.HIGHEST)


def body(orbitals, potential, coefficients, owners, *, bands, domains):
    width = orbitals.shape[0]
    mine = lax.axis_index("band")
    sources = owners // width
    offsets = owners % width
    layers = domains // width

    def part(source):
        return lax.dynamic_slice(coefficients, (source * width, mine * width), (width, width))

    if bands == 2:
        kept, theirs = part(mine), jnp.zeros((width, width), jnp.float32)
        for turn in range(owners.shape[0]):
            rolled = jnp.roll(part(sources[turn]), offsets[turn], axis=0)
            kept = kept + jnp.where(sources[turn] == mine, rolled, 0.0)
            theirs = theirs + jnp.where(sources[turn] == mine, 0.0, rolled)
        mix = jnp.concatenate([kept, theirs], axis=0)
        filtered, rotated = run_filter(orbitals, potential, mix, layers, bands)
        return filtered, rotated
    (filtered,) = run_filter(orbitals, potential, jnp.zeros((8, 4), jnp.float32), layers, bands)
    rotated = mixing(filtered, coefficients, mine, mine, width)
    for turn in range(owners.shape[0]):
        arrived = spread(filtered, "band", sources[turn])
        rolled = jnp.roll(arrived, -offsets[turn], axis=0)
        rotated = rotated + mixing(rolled, coefficients, sources[turn], mine, width)
    return filtered, rotated


def solution(mesh):
    in_specs = (P("band", "domain", None), P("domain", None), P(), P())
    out_specs = (P("band", "domain", None), P("band", "domain", None))
    step = functools.partial(body, bands=mesh.shape["band"], domains=mesh.shape["domain"])
    return jax.shard_map(step, mesh=mesh, in_specs=in_specs, out_specs=out_specs, check_vma=False)
```

```python
import functools

import jax
import jax.numpy as jnp
from jax import lax
from jax.experimental import pallas as pl
from jax.experimental.pallas import tpu as pltpu
from jax.sharding import PartitionSpec as P

LANES = 128
HALO = 4
PAD = 8
MESH = pl.DeviceIdType.MESH

lap_coeffs = (-205.0 / 72.0, 8.0 / 5.0, -1.0 / 5.0, 8.0 / 315.0, -1.0 / 560.0)
CENTER = 6.0
HALF = 5.0


def stencil_planes(out_store, v, prev, pot, rows, stride, first, count):
    weights = [-0.5 * c / HALF for c in lap_coeffs]
    blocks = rows // 24
    lane = lax.broadcasted_iota(jnp.int32, (8, LANES), 1)
    high = lane >= 64
    zero = jnp.zeros((8, LANES), jnp.float32)

    def block(index, carry):
        plane = first + index // blocks
        row = (index % blocks) * 24
        base = PAD + (plane + HALO) * stride + row

        def at(ref, start):
            return ref[pl.ds(start, 8, stride=3), :]

        near = {t: at(v, base + t) for t in range(-6, 9)}
        for t in range(3):
            x = near[t]
            nxt = near[t + 1] if t < 2 else zero
            prv = near[t - 1] if t > 0 else zero
            total = at(pot, plane * rows + row + t) * x
            odd = None
            for k in range(1, 5):
                up, down = lane < k, lane >= LANES - k
                if t == 1:
                    fill_up = jnp.where(high, 0.0, nxt)
                    fill_down = jnp.where(high, prv, 0.0)
                    up = up | (high & (lane < 64 + k))
                    down = down | ((lane >= 64 - k) & (lane < 64))
                else:
                    fill_up, fill_down = nxt, prv
                plus = pltpu.roll(jnp.where(up, fill_up, x), LANES - k, 1)
                minus = pltpu.roll(jnp.where(down, fill_down, x), k, 1)
                pairs = plus + minus
                pairs = pairs + (at(v, base + t + k * stride) + at(v, base + t - k * stride))
                if k % 2 == 0:
                    jump = 3 * k // 2
                    pairs = pairs + (near[t + jump] + near[t - jump])
                else:
                    low_jump = (3 * k) // 2
                    half = jnp.where(
                        high,
                        near[t + low_jump] + near[t - low_jump - 1],
                        near[t + low_jump + 1] + near[t - low_jump],
                    )
                    half = weights[k] * half
                    odd = half if odd is None else odd + half
                total = total + weights[k] * pairs
            total = total + pltpu.roll(odd, 64, 1)
            if prev is not None:
                total = (total + total) - at(prev, base + t)
            out_store(plane, row + t, total)
        return carry

    lax.fori_loop(0, count * blocks, block, 0, unroll=4)


def filter_kernel(
    layers, bands, planes, rows, stride, orbitals, potential, mix, *refs
):
    group = 4
    own = group * planes
    if bands == 2:
        out_f, out_r = refs[:2]
        refs = refs[2:]
    else:
        out_f, out_r = refs[0], None
        refs = refs[1:]
    (v0, v1, v2, v3, pot, stage, pot_stage, recv, local_sem, in_send, in_recv,
     pot_send, pot_recv, halo_send, halo_recv, out_send, out_recv) = refs
    me = lax.axis_index("domain")
    band = lax.axis_index("band")
    g = lax.rem(me, group)
    layer = me // group
    root = layer * group
    left = lax.rem(layer + layers - 1, layers) * group + g
    right = lax.rem(layer + 1, layers) * group + g
    core = root + (g + 1 - 2 * lax.rem(g, 2))
    across = root + lax.rem(g + 2, group)
    g_across = lax.rem(g + 2, group)

    barrier = pltpu.get_barrier_semaphore()
    friends = [(root + lax.rem(g + d, group), band) for d in range(1, group)] + [(left, band), (right, band)]
    if bands == 2:
        friends += [(root + d, 1 - band) for d in range(group)]
    for friend in friends:
        pl.semaphore_signal(barrier, inc=1, device_id=friend, device_id_type=MESH)
    mine_orbital = pltpu.make_async_copy(orbitals.at[g], stage.at[g], local_sem.at[0])
    mine_orbital.start()
    mine_pot = pltpu.make_async_copy(potential, pot_stage.at[g], local_sem.at[1])
    mine_pot.start()
    pl.semaphore_wait(barrier, len(friends))

    def orbital_send(d):
        q = lax.rem(g + d, group)
        return pltpu.make_async_remote_copy(
            orbitals.at[q], stage.at[g], in_send.at[d - 1], in_recv.at[d - 1],
            device_id=(root + q, band), device_id_type=MESH)

    def orbital_arrival(d):
        slot = stage.at[lax.rem(g + group - d, group)]
        pltpu.make_async_copy(slot, slot, in_recv.at[d - 1]).wait()

    for d in (2, 1, 3):
        orbital_send(d).start()

    gap = jnp.zeros((PAD, LANES), jnp.float32)

    def clear(index, carry):
        at = pl.multiple_of((index + HALO) * stride, 8)
        for ref in (v0, v1, v2):
            ref[pl.ds(at, PAD), :] = gap
        return carry

    lax.fori_loop(0, own + 1, clear, 0)

    def spread_planes(source, slot, store):
        def step(tile, carry):
            columns = pl.ds(pl.multiple_of(tile * LANES, LANES), LANES)
            store(tile, source[slot, :, columns])
            return carry

        lax.fori_loop(0, rows, step, 0, unroll=8)

    def unpack_orbital(slot):
        def store(tile, value):
            v0[pl.ds(PAD + (HALO + slot * planes) * stride + tile, planes, stride=stride), :] = value

        spread_planes(stage, slot, store)

    def unpack_pot(slot):
        def store(tile, value):
            scaled = (value - (CENTER + 1.5 * lap_coeffs[0])) * (1.0 / HALF)
            pot[pl.ds(slot * planes * rows + tile, planes, stride=rows), :] = scaled

        spread_planes(pot_stage, slot, store)

    mine_orbital.wait()
    unpack_orbital(g)
    for d in (1, 3, 2):
        orbital_arrival(d)
        unpack_orbital(lax.rem(g + group - d, group))

    length = HALO * stride - PAD
    spots = (PAD, PAD + HALO * stride, PAD + own * stride, PAD + (own + HALO) * stride)

    def halo_copies(level):
        ref = (v0, v1, v2)[level]
        low, first, last, high = (ref.at[pl.ds(s, length), :] for s in spots)
        return (
            pltpu.make_async_remote_copy(
                first, high, halo_send.at[level, 0], halo_recv.at[level, 0],
                device_id=(left, band), device_id_type=MESH),
            pltpu.make_async_remote_copy(
                last, low, halo_send.at[level, 1], halo_recv.at[level, 1],
                device_id=(right, band), device_id_type=MESH),
        )

    def start_halo(level):
        for copy in halo_copies(level):
            copy.start()

    def wait_halo(level):
        for copy in halo_copies(level):
            copy.wait_recv()

    start_halo(0)

    pot_core = pltpu.make_async_remote_copy(
        potential, pot_stage.at[g], pot_send.at[0], pot_recv.at[0], device_id=(core, band), device_id_type=MESH)
    pot_across = pltpu.make_async_remote_copy(
        potential, pot_stage.at[g], pot_send.at[1], pot_recv.at[1], device_id=(across, band), device_id_type=MESH)
    pot_relay = pltpu.make_async_remote_copy(
        pot_stage.at[g_across], pot_stage.at[g_across], pot_send.at[2], pot_recv.at[2],
        device_id=(core, band), device_id_type=MESH)
    pot_across.start()
    pot_core.start()
    g_core = g + 1 - 2 * lax.rem(g, 2)
    mine_pot.wait()
    unpack_pot(g)
    pot_core.wait_recv()
    unpack_pot(g_core)
    pot_across.wait_recv()
    pot_relay.start()
    unpack_pot(g_across)
    pot_relay.wait_recv()
    unpack_pot(lax.rem(g_core + 2, group))

    def padded(ref):
        def store(plane, row, value):
            ref[pl.ds(PAD + (plane + HALO) * stride + row, 8, stride=3), :] = value
        return store

    def plain(plane, row, value):
        v3[pl.ds(plane * rows + row, 8, stride=3), :] = value

    def level(number, first, count):
        if number == 1:
            stencil_planes(padded(v1), v0, None, pot, rows, stride, first, count)
        elif number == 2:
            stencil_planes(padded(v2), v1, v0, pot, rows, stride, first, count)
        else:
            stencil_planes(plain, v2, v1, pot, rows, stride, first, count)

    def piece_span(home, piece):
        start = 2 * (home % 2) if piece == 0 else 4 * (1 - home % 2)
        return start * rows, (4 if piece == 0 else 2) * rows

    def out_copies(home, piece):
        start, size = piece_span(home, piece)
        source = v3.at[pl.ds(home * planes * rows + start, size), :]
        remote = pltpu.make_async_remote_copy(
            source, recv.at[g, pl.ds(start, size), :], out_send.at[0, home, piece], out_recv.at[0, g, piece],
            device_id=(root + home, band), device_id_type=MESH)
        local = pltpu.make_async_copy(
            source, recv.at[g, pl.ds(start, size), :], out_recv.at[0, g, piece])
        peer = None
        if bands == 2:
            peer = pltpu.make_async_remote_copy(
                source, recv.at[group + g, pl.ds(start, size), :], out_send.at[1, home, piece],
                out_recv.at[1, g, piece], device_id=(root + home, 1 - band), device_id_type=MESH)
        return remote, local, peer

    def start_out(home, piece):
        remote, local, peer = out_copies(home, piece)
        if peer is not None:
            peer.start()

        @pl.when(g != home)
        def _():
            remote.start()

        @pl.when(g == home)
        def _():
            local.start()

    level(1, 4, own - 8)
    wait_halo(0)
    level(1, 0, 4)
    level(1, own - 4, 4)
    start_halo(1)
    level(2, 4, own - 8)
    level(3, 8, own - 16)
    start_out(1, 0)
    start_out(2, 0)
    wait_halo(1)
    level(2, 0, 4)
    level(2, own - 4, 4)
    start_halo(2)
    level(3, 4, 4)
    level(3, own - 8, 4)
    for home in range(group):
        start_out(home, 1)
    wait_halo(2)
    level(3, 0, 4)
    level(3, own - 4, 4)
    start_out(0, 0)
    start_out(3, 0)

    mine_start4 = 2 * lax.rem(g, 2) * rows
    mine_start2 = 4 * (1 - lax.rem(g, 2)) * rows
    for peer in range(bands if bands == 2 else 1):
        for q in range(group):
            for piece, start, size in ((0, mine_start4, 4 * rows), (1, mine_start2, 2 * rows)):
                where = recv.at[peer * group + q, pl.ds(pl.multiple_of(start, 8), size), :]
                pltpu.make_async_copy(where, where, out_recv.at[peer, q, piece]).wait()

    def finish(tile, carry):
        columns = pl.ds(pl.multiple_of(tile * LANES, LANES), LANES)
        inputs = [recv[i, pl.ds(tile, planes, stride=rows), :] for i in range(group * (2 if bands == 2 else 1))]
        for i in range(group):
            out_f[i, :, columns] = inputs[i]
        if out_r is not None:
            for c in range(group):
                total = mix[0, c] * inputs[0]
                for i in range(1, 2 * group):
                    total = total + mix[i, c] * inputs[i]
                out_r[c, :, columns] = total
        return carry

    lax.fori_loop(0, rows, finish, 0, unroll=2)

    for d in range(1, group):
        orbital_send(d).wait_send()
    for copy in (pot_core, pot_across, pot_relay):
        copy.wait_send()
    for number in range(3):
        for copy in halo_copies(number):
            copy.wait_send()
    for home in range(group):
        for piece in range(2):
            remote, local, peer = out_copies(home, piece)
            if peer is not None:
                peer.wait_send()

            @pl.when(g != home)
            def _():
                remote.wait_send()


def run_filter(orbitals, potential, mix, layers, bands):
    width, planes, cells = orbitals.shape
    rows = cells // LANES
    stride = rows + PAD
    own = width * planes
    padded_rows = (own + 2 * HALO) * stride + PAD
    f32 = jnp.float32
    count = 2 if bands == 2 else 1
    dma = pltpu.SemaphoreType.DMA
    shape = jax.ShapeDtypeStruct(orbitals.shape, f32)
    any_spec = pl.BlockSpec(memory_space=pl.ANY)
    return pl.pallas_call(
        functools.partial(filter_kernel, layers, bands, planes, rows, stride),
        out_shape=[shape] * count,
        in_specs=[any_spec, any_spec, pl.BlockSpec(memory_space=pltpu.SMEM)],
        out_specs=[pl.BlockSpec(memory_space=pltpu.VMEM)] * count,
        scratch_shapes=[
            pltpu.VMEM((padded_rows, LANES), f32),
            pltpu.VMEM((padded_rows, LANES), f32),
            pltpu.VMEM((padded_rows, LANES), f32),
            pltpu.VMEM((own * rows, LANES), f32),
            pltpu.VMEM((own * rows, LANES), f32),
            pltpu.VMEM((width, planes, cells), f32),
            pltpu.VMEM((width, planes, cells), f32),
            pltpu.VMEM((count * width, planes * rows, LANES), f32),
            dma((2,)), dma((3,)), dma((3,)), dma((3,)), dma((3,)),
            dma((3, 2)), dma((3, 2)), dma((2, 4, 2)), dma((2, 4, 2)),
        ],
        compiler_params=pltpu.CompilerParams(
            collective_id=0, has_side_effects=True, vmem_limit_bytes=60 * 1024 * 1024
        ),
    )(orbitals, potential, mix)


def spread(value, axis, source):
    kept = jnp.where(lax.axis_index(axis) == source, value, 0).astype(value.dtype)
    return lax.psum(kept, axis)


def mixing(block, coefficients, source, target, width):
    part_coeffs = lax.dynamic_slice(coefficients, (source * width, target * width), (width, width))
    return jnp.einsum("bxp,bc->cxp", block, part_coeffs, precision=lax.Precision.HIGHEST)


def body(orbitals, potential, coefficients, owners, *, bands, domains):
    width = orbitals.shape[0]
    mine = lax.axis_index("band")
    sources = owners // width
    offsets = owners % width
    layers = domains // width

    def part(source):
        return lax.dynamic_slice(coefficients, (source * width, mine * width), (width, width))

    if bands == 2:
        kept, theirs = part(mine), jnp.zeros((width, width), jnp.float32)
        for turn in range(owners.shape[0]):
            rolled = jnp.roll(part(sources[turn]), offsets[turn], axis=0)
            kept = kept + jnp.where(sources[turn] == mine, rolled, 0.0)
            theirs = theirs + jnp.where(sources[turn] == mine, 0.0, rolled)
        mix = jnp.concatenate([kept, theirs], axis=0)
        filtered, rotated = run_filter(orbitals, potential, mix, layers, bands)
        return filtered, rotated
    (filtered,) = run_filter(orbitals, potential, jnp.zeros((8, 4), jnp.float32), layers, bands)
    rotated = mixing(filtered, coefficients, mine, mine, width)
    for turn in range(owners.shape[0]):
        arrived = spread(filtered, "band", sources[turn])
        rolled = jnp.roll(arrived, -offsets[turn], axis=0)
        rotated = rotated + mixing(rolled, coefficients, sources[turn], mine, width)
    return filtered, rotated


def solution(mesh):
    in_specs = (P("band", "domain", None), P("domain", None), P(), P())
    out_specs = (P("band", "domain", None), P("band", "domain", None))
    step = functools.partial(body, bands=mesh.shape["band"], domains=mesh.shape["domain"])
    return jax.shard_map(step, mesh=mesh, in_specs=in_specs, out_specs=out_specs, check_vma=False)
```

```python
import functools

import jax
import jax.numpy as jnp
from jax import lax
from jax.experimental import pallas as pl
from jax.experimental.pallas import tpu as pltpu
from jax.sharding import PartitionSpec as P

LANES = 128
HALO = 4
PAD = 8
MESH = pl.DeviceIdType.MESH

lap_coeffs = (-205.0 / 72.0, 8.0 / 5.0, -1.0 / 5.0, 8.0 / 315.0, -1.0 / 560.0)
CENTER = 6.0
HALF = 5.0


def stencil_planes(out_store, v, prev, pot, rows, stride, first, count):
    weights = [-0.5 * c / HALF for c in lap_coeffs]
    blocks = rows // 24
    lane = lax.broadcasted_iota(jnp.int32, (8, LANES), 1)
    high = lane >= 64
    zero = jnp.zeros((8, LANES), jnp.float32)

    def block(plane, row):
        base = PAD + (plane + HALO) * stride + row
        here = plane * rows + row

        def at(ref, start):
            return ref[pl.ds(start, 8, stride=3), :]

        near = {t: at(v, base + t) for t in range(-6, 9)}
        for t in range(3):
            x = near[t]
            nxt = near[t + 1] if t < 2 else zero
            prv = near[t - 1] if t > 0 else zero
            total = at(pot, here + t) * x
            odd = None
            for k in range(1, 5):
                up, down = lane < k, lane >= LANES - k
                if t == 1:
                    fill_up = jnp.where(high, 0.0, nxt)
                    fill_down = jnp.where(high, prv, 0.0)
                    up = up | (high & (lane < 64 + k))
                    down = down | ((lane >= 64 - k) & (lane < 64))
                else:
                    fill_up, fill_down = nxt, prv
                plus = pltpu.roll(jnp.where(up, fill_up, x), LANES - k, 1)
                minus = pltpu.roll(jnp.where(down, fill_down, x), k, 1)
                pairs = plus + minus
                pairs = pairs + (at(v, base + t + k * stride) + at(v, base + t - k * stride))
                if k % 2 == 0:
                    jump = 3 * k // 2
                    pairs = pairs + (near[t + jump] + near[t - jump])
                else:
                    low_jump = (3 * k) // 2
                    half = jnp.where(
                        high,
                        near[t + low_jump] + near[t - low_jump - 1],
                        near[t + low_jump + 1] + near[t - low_jump],
                    )
                    half = weights[k] * half
                    odd = half if odd is None else odd + half
                total = total + weights[k] * pairs
            total = total + pltpu.roll(odd, 64, 1)
            if prev is not None:
                total = (total + total) - at(prev, base + t)
            out_store(plane, row + t, total)

    def one_plane(index, carry):
        for number in range(blocks):
            block(first + index, number * 24)
        return carry

    lax.fori_loop(0, count, one_plane, 0)


def filter_kernel(
    layers, bands, planes, rows, stride, orbitals, potential, mix, *refs
):
    group = 4
    own = group * planes
    if bands == 2:
        out_f, out_r = refs[:2]
        refs = refs[2:]
    else:
        out_f, out_r = refs[0], None
        refs = refs[1:]
    (v0, v1, v2, v3, pot, loaded, packed, pot_stage, recv, local_sem, in_send, in_recv,
     pot_send, pot_recv, halo_send, halo_recv, out_send, out_recv) = refs
    me = lax.axis_index("domain")
    band = lax.axis_index("band")
    g = lax.rem(me, group)
    layer = me // group
    root = layer * group
    left = lax.rem(layer + layers - 1, layers) * group + g
    right = lax.rem(layer + 1, layers) * group + g
    core = root + (g + 1 - 2 * lax.rem(g, 2))
    across = root + lax.rem(g + 2, group)
    g_across = lax.rem(g + 2, group)

    load = pltpu.make_async_copy(orbitals, loaded, local_sem.at[0])
    load.start()
    mine_pot = pltpu.make_async_copy(potential, pot_stage.at[g], local_sem.at[1])
    mine_pot.start()

    gap = jnp.zeros((PAD, LANES), jnp.float32)

    def clear(index, carry):
        at = pl.multiple_of((index + HALO) * stride, 8)
        for ref in (v0, v1, v2):
            ref[pl.ds(at, PAD), :] = gap
        return carry

    lax.fori_loop(0, own + 1, clear, 0)
    for index in range(own):
        packed[pl.ds(index * stride + rows, PAD), :] = gap

    barrier = pltpu.get_barrier_semaphore()
    friends = [(root + lax.rem(g + d, group), band) for d in range(1, group)] + [(left, band), (right, band)]
    if bands == 2:
        friends += [(root + d, 1 - band) for d in range(group)]
    for friend in friends:
        pl.semaphore_signal(barrier, inc=1, device_id=friend, device_id_type=MESH)
    load.wait()

    def pack(index, carry):
        for plane in range(planes):
            for q in range(group):
                value = loaded[pl.ds((plane * rows + index * 8) * group + q, 8, stride=group), :]
                at = pl.multiple_of((q * planes + plane) * stride + index * 8, 8)
                packed[pl.ds(at, 8), :] = value
        return carry

    lax.fori_loop(0, rows // 8, pack, 0)
    pl.semaphore_wait(barrier, len(friends))
    share = planes * stride - PAD

    def home_slot(q):
        return v0.at[pl.ds(pl.multiple_of(PAD + (HALO + q * planes) * stride, 8), share), :]

    def orbital_source(q):
        return packed.at[pl.ds(pl.multiple_of(q * planes * stride, 8), share), :]

    def orbital_send(d):
        q = lax.rem(g + d, group)
        return pltpu.make_async_remote_copy(
            orbital_source(q), home_slot(g), in_send.at[d - 1], in_recv.at[d - 1],
            device_id=(root + q, band), device_id_type=MESH)

    def orbital_arrival(d):
        slot = home_slot(lax.rem(g + group - d, group))
        pltpu.make_async_copy(slot, slot, in_recv.at[d - 1]).wait()

    for d in (2, 1, 3):
        orbital_send(d).start()
    mine_orbital = pltpu.make_async_copy(orbital_source(g), home_slot(g), local_sem.at[2])
    mine_orbital.start()

    def spread_planes(source, slot, store):
        def step(tile, carry):
            columns = pl.ds(pl.multiple_of(tile * LANES, LANES), LANES)
            store(tile, source[slot, :, columns])
            return carry

        lax.fori_loop(0, rows, step, 0, unroll=8)

    def unpack_pot(slot):
        def store(tile, value):
            scaled = (value - (CENTER + 1.5 * lap_coeffs[0])) * (1.0 / HALF)
            pot[pl.ds(slot * planes * rows + tile, planes, stride=rows), :] = scaled

        spread_planes(pot_stage, slot, store)

    mine_orbital.wait()
    for d in (1, 3, 2):
        orbital_arrival(d)

    length = HALO * stride - PAD
    spots = (PAD, PAD + HALO * stride, PAD + own * stride, PAD + (own + HALO) * stride)

    def halo_copies(level):
        ref = (v0, v1, v2)[level]
        low, first, last, high = (ref.at[pl.ds(s, length), :] for s in spots)
        return (
            pltpu.make_async_remote_copy(
                first, high, halo_send.at[level, 0], halo_recv.at[level, 0],
                device_id=(left, band), device_id_type=MESH),
            pltpu.make_async_remote_copy(
                last, low, halo_send.at[level, 1], halo_recv.at[level, 1],
                device_id=(right, band), device_id_type=MESH),
        )

    def start_halo(level):
        for copy in halo_copies(level):
            copy.start()

    def wait_halo(level):
        for copy in halo_copies(level):
            copy.wait_recv()

    start_halo(0)

    pot_core = pltpu.make_async_remote_copy(
        potential, pot_stage.at[g], pot_send.at[0], pot_recv.at[0], device_id=(core, band), device_id_type=MESH)
    pot_across = pltpu.make_async_remote_copy(
        potential, pot_stage.at[g], pot_send.at[1], pot_recv.at[1], device_id=(across, band), device_id_type=MESH)
    pot_relay = pltpu.make_async_remote_copy(
        pot_stage.at[g_across], pot_stage.at[g_across], pot_send.at[2], pot_recv.at[2],
        device_id=(core, band), device_id_type=MESH)
    pot_across.start()
    pot_core.start()
    g_core = g + 1 - 2 * lax.rem(g, 2)
    mine_pot.wait()
    unpack_pot(g)
    pot_core.wait_recv()
    unpack_pot(g_core)
    pot_across.wait_recv()
    pot_relay.start()
    unpack_pot(g_across)
    pot_relay.wait_recv()
    unpack_pot(lax.rem(g_core + 2, group))

    def padded(ref):
        def store(plane, row, value):
            ref[pl.ds(PAD + (plane + HALO) * stride + row, 8, stride=3), :] = value
        return store

    def plain(plane, row, value):
        v3[pl.ds(plane * rows + row, 8, stride=3), :] = value

    def level(number, first, count):
        if number == 1:
            stencil_planes(padded(v1), v0, None, pot, rows, stride, first, count)
        elif number == 2:
            stencil_planes(padded(v2), v1, v0, pot, rows, stride, first, count)
        else:
            stencil_planes(plain, v2, v1, pot, rows, stride, first, count)

    share_rows = planes * rows

    def piece_span(home, piece):
        start = 2 * (home % 2) if piece == 0 else 4 * (1 - home % 2)
        return start * rows, (4 if piece == 0 else 2) * rows

    def out_copies(home, piece):
        start, size = piece_span(home, piece)
        source = v3.at[pl.ds(home * planes * rows + start, size), :]
        remote = pltpu.make_async_remote_copy(
            source, recv.at[pl.ds(pl.multiple_of(g * share_rows + start, 8), size), :], out_send.at[0, home, piece], out_recv.at[0, g, piece],
            device_id=(root + home, band), device_id_type=MESH)
        local = pltpu.make_async_copy(
            source, recv.at[pl.ds(pl.multiple_of(g * share_rows + start, 8), size), :], out_recv.at[0, g, piece])
        peer = None
        if bands == 2:
            peer = pltpu.make_async_remote_copy(
                source, recv.at[pl.ds(pl.multiple_of((group + g) * share_rows + start, 8), size), :], out_send.at[1, home, piece],
                out_recv.at[1, g, piece], device_id=(root + home, 1 - band), device_id_type=MESH)
        return remote, local, peer

    def start_out(home, piece):
        remote, local, peer = out_copies(home, piece)
        if peer is not None:
            peer.start()

        @pl.when(g != home)
        def _():
            remote.start()

        @pl.when(g == home)
        def _():
            local.start()

    level(1, 4, own - 8)
    wait_halo(0)
    level(1, 0, 4)
    level(1, own - 4, 4)
    start_halo(1)
    level(2, 4, own - 8)
    level(3, 8, own - 16)
    start_out(1, 0)
    start_out(2, 0)
    wait_halo(1)
    level(2, 0, 4)
    level(2, own - 4, 4)
    start_halo(2)
    level(3, 4, 4)
    level(3, own - 8, 4)
    for home in range(group):
        start_out(home, 1)
    wait_halo(2)
    level(3, 0, 4)
    level(3, own - 4, 4)
    start_out(0, 0)
    start_out(3, 0)

    mine_start4 = 2 * lax.rem(g, 2) * rows
    mine_start2 = 4 * (1 - lax.rem(g, 2)) * rows
    for peer in range(bands if bands == 2 else 1):
        for q in range(group):
            for piece, start, size in ((0, mine_start4, 4 * rows), (1, mine_start2, 2 * rows)):
                where = recv.at[pl.ds(pl.multiple_of((peer * group + q) * share_rows + start, 8), size), :]
                pltpu.make_async_copy(where, where, out_recv.at[peer, q, piece]).wait()

    def finish(index, carry):
        at = index * 8
        inputs = [
            recv[pl.ds(pl.multiple_of(i * share_rows + at, 8), 8), :]
            for i in range(group * (2 if bands == 2 else 1))
        ]
        for i in range(group):
            out_f[pl.ds(at * group + i, 8, stride=group), :] = inputs[i]
        if out_r is not None:
            for c in range(group):
                total = mix[0, c] * inputs[0]
                for i in range(1, 2 * group):
                    total = total + mix[i, c] * inputs[i]
                out_r[pl.ds(at * group + c, 8, stride=group), :] = total
        return carry

    lax.fori_loop(0, share_rows // 8, finish, 0, unroll=4)

    for d in range(1, group):
        orbital_send(d).wait_send()
    for copy in (pot_core, pot_across, pot_relay):
        copy.wait_send()
    for number in range(3):
        for copy in halo_copies(number):
            copy.wait_send()
    for home in range(group):
        for piece in range(2):
            remote, local, peer = out_copies(home, piece)
            if peer is not None:
                peer.wait_send()

            @pl.when(g != home)
            def _():
                remote.wait_send()


def run_filter(orbitals, potential, mix, layers, bands):
    width, planes, cells = orbitals.shape
    rows = cells // LANES
    stride = rows + PAD
    own = width * planes
    padded_rows = (own + 2 * HALO) * stride + PAD
    f32 = jnp.float32
    count = 2 if bands == 2 else 1
    dma = pltpu.SemaphoreType.DMA
    shape = jax.ShapeDtypeStruct((own * rows, LANES), f32)
    any_spec = pl.BlockSpec(memory_space=pl.ANY)
    interleaved = orbitals.transpose(1, 0, 2).reshape(planes, width, rows, LANES)
    interleaved = interleaved.transpose(0, 2, 1, 3).reshape(own * rows, LANES)
    outs = pl.pallas_call(
        functools.partial(filter_kernel, layers, bands, planes, rows, stride),
        out_shape=[shape] * count,
        in_specs=[any_spec, any_spec, pl.BlockSpec(memory_space=pltpu.SMEM)],
        out_specs=[pl.BlockSpec(memory_space=pltpu.VMEM)] * count,
        scratch_shapes=[
            pltpu.VMEM((padded_rows, LANES), f32),
            pltpu.VMEM((padded_rows, LANES), f32),
            pltpu.VMEM((padded_rows, LANES), f32),
            pltpu.VMEM((own * rows, LANES), f32),
            pltpu.VMEM((own * rows, LANES), f32),
            pltpu.VMEM((own * rows, LANES), f32),
            pltpu.VMEM((own * stride, LANES), f32),
            pltpu.VMEM((width, planes, cells), f32),
            pltpu.VMEM((count * own * rows, LANES), f32),
            dma((3,)), dma((3,)), dma((3,)), dma((3,)), dma((3,)),
            dma((3, 2)), dma((3, 2)), dma((2, 4, 2)), dma((2, 4, 2)),
        ],
        compiler_params=pltpu.CompilerParams(
            collective_id=0, has_side_effects=True, vmem_limit_bytes=60 * 1024 * 1024
        ),
    )(interleaved, potential, mix)

    def whole(flat):
        apart = flat.reshape(planes, rows, width, LANES).transpose(0, 2, 1, 3)
        return apart.reshape(planes, width, cells).transpose(1, 0, 2)

    return [whole(flat) for flat in outs]


def spread(value, axis, source):
    kept = jnp.where(lax.axis_index(axis) == source, value, 0).astype(value.dtype)
    return lax.psum(kept, axis)


def mixing(block, coefficients, source, target, width):
    part_coeffs = lax.dynamic_slice(coefficients, (source * width, target * width), (width, width))
    return jnp.einsum("bxp,bc->cxp", block, part_coeffs, precision=lax.Precision.HIGHEST)


def body(orbitals, potential, coefficients, owners, *, bands, domains):
    width = orbitals.shape[0]
    mine = lax.axis_index("band")
    sources = owners // width
    offsets = owners % width
    layers = domains // width

    def part(source):
        return lax.dynamic_slice(coefficients, (source * width, mine * width), (width, width))

    if bands == 2:
        kept, theirs = part(mine), jnp.zeros((width, width), jnp.float32)
        for turn in range(owners.shape[0]):
            rolled = jnp.roll(part(sources[turn]), offsets[turn], axis=0)
            kept = kept + jnp.where(sources[turn] == mine, rolled, 0.0)
            theirs = theirs + jnp.where(sources[turn] == mine, 0.0, rolled)
        mix = jnp.concatenate([kept, theirs], axis=0)
        filtered, rotated = run_filter(orbitals, potential, mix, layers, bands)
        return filtered, rotated
    (filtered,) = run_filter(orbitals, potential, jnp.zeros((8, 4), jnp.float32), layers, bands)
    rotated = mixing(filtered, coefficients, mine, mine, width)
    for turn in range(owners.shape[0]):
        arrived = spread(filtered, "band", sources[turn])
        rolled = jnp.roll(arrived, -offsets[turn], axis=0)
        rotated = rotated + mixing(rolled, coefficients, sources[turn], mine, width)
    return filtered, rotated


def solution(mesh):
    in_specs = (P("band", "domain", None), P("domain", None), P(), P())
    out_specs = (P("band", "domain", None), P("band", "domain", None))
    step = functools.partial(body, bands=mesh.shape["band"], domains=mesh.shape["domain"])
    return jax.shard_map(step, mesh=mesh, in_specs=in_specs, out_specs=out_specs, check_vma=False)
```

```python
import functools

import jax
import jax.numpy as jnp
from jax import lax
from jax.experimental import pallas as pl
from jax.experimental.pallas import tpu as pltpu
from jax.sharding import PartitionSpec as P

LANES = 128
HALO = 4
PAD = 8
MESH = pl.DeviceIdType.MESH

lap_coeffs = (-205.0 / 72.0, 8.0 / 5.0, -1.0 / 5.0, 8.0 / 315.0, -1.0 / 560.0)
CENTER = 6.0
HALF = 5.0


def stencil_planes(out_store, v, prev, pot, rows, stride, first, count):
    weights = [-0.5 * c / HALF for c in lap_coeffs]
    blocks = rows // 24
    lane = lax.broadcasted_iota(jnp.int32, (8, LANES), 1)
    high = lane >= 64
    zero = jnp.zeros((8, LANES), jnp.float32)

    def block(plane, row):
        base = PAD + (plane + HALO) * stride + row
        here = plane * rows + row

        def at(ref, start):
            return ref[pl.ds(start, 8, stride=3), :]

        near = {t: at(v, base + t) for t in range(-6, 9)}
        for t in range(3):
            x = near[t]
            nxt = near[t + 1] if t < 2 else zero
            prv = near[t - 1] if t > 0 else zero
            total = at(pot, here + t) * x
            odd = None
            for k in range(1, 5):
                up, down = lane < k, lane >= LANES - k
                if t == 1:
                    fill_up = jnp.where(high, 0.0, nxt)
                    fill_down = jnp.where(high, prv, 0.0)
                    up = up | (high & (lane < 64 + k))
                    down = down | ((lane >= 64 - k) & (lane < 64))
                else:
                    fill_up, fill_down = nxt, prv
                plus = pltpu.roll(jnp.where(up, fill_up, x), LANES - k, 1)
                minus = pltpu.roll(jnp.where(down, fill_down, x), k, 1)
                pairs = plus + minus
                pairs = pairs + (at(v, base + t + k * stride) + at(v, base + t - k * stride))
                if k % 2 == 0:
                    jump = 3 * k // 2
                    pairs = pairs + (near[t + jump] + near[t - jump])
                else:
                    low_jump = (3 * k) // 2
                    half = jnp.where(
                        high,
                        near[t + low_jump] + near[t - low_jump - 1],
                        near[t + low_jump + 1] + near[t - low_jump],
                    )
                    half = weights[k] * half
                    odd = half if odd is None else odd + half
                total = total + weights[k] * pairs
            total = total + pltpu.roll(odd, 64, 1)
            if prev is not None:
                total = (total + total) - at(prev, base + t)
            out_store(plane, row + t, total)

    def one_plane(index, carry):
        for number in range(blocks):
            block(first + index, number * 24)
        return carry

    lax.fori_loop(0, count, one_plane, 0)


def filter_kernel(
    layers, bands, planes, rows, stride, orbitals, potential, recv, *refs
):
    group = 4
    own = group * planes
    (v0, v1, v2, v3, pot, go_sem, loaded, packed, pot_stage, local_sem, in_send, in_recv,
     pot_send, pot_recv, halo_send, halo_recv, out_send, out_recv) = refs
    me = lax.axis_index("domain")
    band = lax.axis_index("band")
    g = lax.rem(me, group)
    layer = me // group
    root = layer * group
    left = lax.rem(layer + layers - 1, layers) * group + g
    right = lax.rem(layer + 1, layers) * group + g
    core = root + (g + 1 - 2 * lax.rem(g, 2))
    g_core = g + 1 - 2 * lax.rem(g, 2)
    g_across = lax.rem(g + 2, group)
    g_diag = lax.rem(g_core + 2, group)
    across = root + g_across
    outer = (g == 0) | (g == group - 1)
    inner = (g == 1) | (g == 2)

    load = pltpu.make_async_copy(orbitals, loaded, local_sem.at[0])
    load.start()
    mine_pot = pltpu.make_async_copy(potential, pot_stage.at[g], local_sem.at[1])
    mine_pot.start()

    gap = jnp.zeros((PAD, LANES), jnp.float32)

    def clear(index, carry):
        at = pl.multiple_of((index + HALO) * stride, 8)
        for ref in (v0, v1, v2):
            ref[pl.ds(at, PAD), :] = gap
        return carry

    lax.fori_loop(0, own + 1, clear, 0)
    for index in range(own):
        packed[pl.ds(index * stride + rows, PAD), :] = gap

    barrier = pltpu.get_barrier_semaphore()
    friends = [(root + lax.rem(g + d, group), band) for d in range(1, group)] + [(left, band), (right, band)]
    if bands == 2:
        friends += [(root + d, 1 - band) for d in range(group)]
    for friend in friends:
        pl.semaphore_signal(barrier, inc=1, device_id=friend, device_id_type=MESH)
    load.wait()

    def pack(index, carry):
        for plane in range(planes):
            for q in range(group):
                value = loaded[pl.ds((plane * rows + index * 8) * group + q, 8, stride=group), :]
                at = pl.multiple_of((q * planes + plane) * stride + index * 8, 8)
                packed[pl.ds(at, 8), :] = value
        return carry

    lax.fori_loop(0, rows // 8, pack, 0)
    pl.semaphore_wait(barrier, len(friends))
    share = planes * stride - PAD

    def home_slot(q):
        return v0.at[pl.ds(pl.multiple_of(PAD + (HALO + q * planes) * stride, 8), share), :]

    def orbital_source(q):
        return packed.at[pl.ds(pl.multiple_of(q * planes * stride, 8), share), :]

    def orbital_send(partner):
        q = (g, g_core, g_across, g_diag)[partner]
        return pltpu.make_async_remote_copy(
            orbital_source(q), home_slot(g), in_send.at[partner], in_recv.at[partner],
            device_id=(root + q, band), device_id_type=MESH)

    def orbital_arrival(partner, slot):
        where = home_slot(slot)
        pltpu.make_async_copy(where, where, in_recv.at[partner]).wait()

    length = HALO * stride - PAD
    spots = (PAD, PAD + HALO * stride, PAD + own * stride, PAD + (own + HALO) * stride)

    def halo_copies(level):
        ref = (v0, v1, v2)[level]
        low, first, last, high = (ref.at[pl.ds(s, length), :] for s in spots)
        return (
            pltpu.make_async_remote_copy(
                first, high, halo_send.at[level, 0], halo_recv.at[level, 0],
                device_id=(left, band), device_id_type=MESH),
            pltpu.make_async_remote_copy(
                last, low, halo_send.at[level, 1], halo_recv.at[level, 1],
                device_id=(right, band), device_id_type=MESH),
        )

    def start_halo(level):
        for copy in halo_copies(level):
            copy.start()

    def wait_halo(level):
        for copy in halo_copies(level):
            copy.wait_recv()

    pot_core = pltpu.make_async_remote_copy(
        potential, pot_stage.at[g], pot_send.at[1], pot_recv.at[1], device_id=(core, band), device_id_type=MESH)
    pot_across = pltpu.make_async_remote_copy(
        potential, pot_stage.at[g], pot_send.at[2], pot_recv.at[2], device_id=(across, band), device_id_type=MESH)
    pot_relay = pltpu.make_async_remote_copy(
        pot_stage.at[g_across], pot_stage.at[g_across], pot_send.at[3], pot_recv.at[3],
        device_id=(core, band), device_id_type=MESH)

    orbital_send(1).start()
    mine_orbital = pltpu.make_async_copy(orbital_source(g), home_slot(g), in_recv.at[0])
    mine_orbital.start()

    @pl.when(outer)
    def _():
        orbital_send(2).start()
        orbital_send(3).start()

    pot_core.start()
    lower = g < 2

    @pl.when(lower)
    def _():
        orbital_arrival(g, 0)
        halo_copies(0)[0].start()

    @pl.when(jnp.logical_not(lower))
    def _():
        orbital_arrival(group - 1 - g, group - 1)
        halo_copies(0)[1].start()

    @pl.when(outer)
    def _():
        orbital_send(2).wait_send()
        orbital_send(3).wait_send()
        pl.semaphore_signal(go_sem, inc=1, device_id=(core, band), device_id_type=MESH)
        pot_across.start()

    @pl.when(inner)
    def _():
        pl.semaphore_wait(go_sem, 1)
        orbital_send(2).start()
        orbital_send(3).start()

    @pl.when(lower)
    def _():
        orbital_arrival(group - 1 - g, group - 1)
        halo_copies(0)[1].start()

    @pl.when(jnp.logical_not(lower))
    def _():
        orbital_arrival(g, 0)
        halo_copies(0)[0].start()

    @pl.when(inner)
    def _():
        orbital_send(2).wait_send()
        orbital_send(3).wait_send()
        pot_across.start()

    def spread_planes(source, slot, store):
        def step(tile, carry):
            columns = pl.ds(pl.multiple_of(tile * LANES, LANES), LANES)
            store(tile, source[slot, :, columns])
            return carry

        lax.fori_loop(0, rows, step, 0, unroll=8)

    def unpack_pot(slot):
        def store(tile, value):
            scaled = (value - (CENTER + 1.5 * lap_coeffs[0])) * (1.0 / HALF)
            pot[pl.ds(slot * planes * rows + tile, planes, stride=rows), :] = scaled

        spread_planes(pot_stage, slot, store)

    def pot_arrival(partner, slot):
        where = pot_stage.at[slot]
        pltpu.make_async_copy(where, where, pot_recv.at[partner]).wait()
        unpack_pot(slot)

    mine_pot.wait()
    unpack_pot(g)
    pot_arrival(1, g_core)

    @pl.when(inner)
    def _():
        pot_across.wait_recv()
        pot_relay.start()

    @pl.when(outer)
    def _():
        pot_relay.wait_recv()

    unpack_pot(jnp.where(inner, g_across, g_diag))

    orbital_arrival(g_core, 1)
    orbital_arrival(lax.rem(g + 2, group), 2)

    def padded(ref):
        def store(plane, row, value):
            ref[pl.ds(PAD + (plane + HALO) * stride + row, 8, stride=3), :] = value
        return store

    def plain(plane, row, value):
        v3[pl.ds(plane * rows + row, 8, stride=3), :] = value

    def level(number, first, count):
        if number == 1:
            stencil_planes(padded(v1), v0, None, pot, rows, stride, first, count)
        elif number == 2:
            stencil_planes(padded(v2), v1, v0, pot, rows, stride, first, count)
        else:
            stencil_planes(plain, v2, v1, pot, rows, stride, first, count)

    share_rows = planes * rows

    def piece_span(home, piece):
        start = 2 * (home % 2) if piece == 0 else 4 * (1 - home % 2)
        return start * rows, (4 if piece == 0 else 2) * rows

    def out_copies(home, piece):
        start, size = piece_span(home, piece)
        source = v3.at[pl.ds(home * planes * rows + start, size), :]
        remote = pltpu.make_async_remote_copy(
            source, recv.at[pl.ds(pl.multiple_of(g * share_rows + start, 8), size), :], out_send.at[0, home, piece], out_recv.at[0, g, piece],
            device_id=(root + home, band), device_id_type=MESH)
        local = pltpu.make_async_copy(
            source, recv.at[pl.ds(pl.multiple_of(g * share_rows + start, 8), size), :], out_recv.at[0, g, piece])
        peer = None
        if bands == 2:
            peer = pltpu.make_async_remote_copy(
                source, recv.at[pl.ds(pl.multiple_of((group + g) * share_rows + start, 8), size), :], out_send.at[1, home, piece],
                out_recv.at[1, g, piece], device_id=(root + home, 1 - band), device_id_type=MESH)
        return remote, local, peer

    def start_out(home, piece):
        remote, local, peer = out_copies(home, piece)
        if peer is not None:
            peer.start()

        @pl.when(g != home)
        def _():
            remote.start()

        @pl.when(g == home)
        def _():
            local.start()

    wait_halo(0)
    level(1, 0, 4)
    level(1, own - 4, 4)
    start_halo(1)

    @pl.when(inner)
    def _():
        pot_relay.wait_recv()

    @pl.when(outer)
    def _():
        pot_across.wait_recv()
        pot_relay.start()

    unpack_pot(jnp.where(inner, g_diag, g_across))
    level(1, 4, own - 8)
    level(2, 4, own - 8)
    level(3, 8, own - 16)
    start_out(1, 0)
    start_out(2, 0)
    wait_halo(1)
    level(2, 0, 4)
    level(2, own - 4, 4)
    start_halo(2)
    level(3, 4, 4)
    level(3, own - 8, 4)
    for home in range(group):
        start_out(home, 1)
    wait_halo(2)
    level(3, 0, 4)
    level(3, own - 4, 4)
    start_out(0, 0)
    start_out(3, 0)

    mine_start4 = 2 * lax.rem(g, 2) * rows
    mine_start2 = 4 * (1 - lax.rem(g, 2)) * rows
    for peer in range(bands if bands == 2 else 1):
        for q in range(group):
            for piece, start, size in ((0, mine_start4, 4 * rows), (1, mine_start2, 2 * rows)):
                where = recv.at[pl.ds(pl.multiple_of((peer * group + q) * share_rows + start, 8), size), :]
                pltpu.make_async_copy(where, where, out_recv.at[peer, q, piece]).wait()

    orbital_send(1).wait_send()
    for copy in (pot_core, pot_across, pot_relay):
        copy.wait_send()
    for number in range(3):
        for copy in halo_copies(number):
            copy.wait_send()
    for home in range(group):
        for piece in range(2):
            remote, local, peer = out_copies(home, piece)
            if peer is not None:
                peer.wait_send()

            @pl.when(g != home)
            def _():
                remote.wait_send()


def run_filter(orbitals, potential, layers, bands):
    width, planes, cells = orbitals.shape
    rows = cells // LANES
    stride = rows + PAD
    own = width * planes
    padded_rows = (own + 2 * HALO) * stride + PAD
    f32 = jnp.float32
    count = 2 if bands == 2 else 1
    dma = pltpu.SemaphoreType.DMA
    shape = jax.ShapeDtypeStruct((count * own * rows, LANES), f32)
    any_spec = pl.BlockSpec(memory_space=pl.ANY)
    interleaved = orbitals.transpose(1, 0, 2).reshape(planes, width, rows, LANES)
    interleaved = interleaved.transpose(0, 2, 1, 3).reshape(own * rows, LANES)
    return pl.pallas_call(
        functools.partial(filter_kernel, layers, bands, planes, rows, stride),
        out_shape=shape,
        in_specs=[any_spec, any_spec],
        out_specs=any_spec,
        scratch_shapes=[
            pltpu.VMEM((padded_rows, LANES), f32),
            pltpu.VMEM((padded_rows, LANES), f32),
            pltpu.VMEM((padded_rows, LANES), f32),
            pltpu.VMEM((own * rows, LANES), f32),
            pltpu.VMEM((own * rows, LANES), f32),
            pltpu.SemaphoreType.REGULAR,
            pltpu.VMEM((own * rows, LANES), f32),
            pltpu.VMEM((own * stride, LANES), f32),
            pltpu.VMEM((width, planes, cells), f32),
            dma((2,)), dma((4,)), dma((4,)), dma((4,)), dma((4,)),
            dma((3, 2)), dma((3, 2)), dma((2, 4, 2)), dma((2, 4, 2)),
        ],
        compiler_params=pltpu.CompilerParams(
            collective_id=0, has_side_effects=True, vmem_limit_bytes=60 * 1024 * 1024
        ),
    )(interleaved, potential)


def rotate_kernel(width, mix, fields, out_f, out_r):
    def group_rows(index, carry):
        at = pl.multiple_of(index * 8, 8)
        inputs = [fields[i, pl.ds(at, 8), :] for i in range(2 * width)]
        for c in range(width):
            out_f[pl.ds(at * width + c, 8, stride=width), :] = inputs[c]
            total = mix[0, c] * inputs[0]
            for i in range(1, 2 * width):
                total = total + mix[i, c] * inputs[i]
            out_r[pl.ds(at * width + c, 8, stride=width), :] = total
        return carry

    lax.fori_loop(0, fields.shape[1] // 8, group_rows, 0, unroll=6)


def run_rotation(fields, mix, width, planes, cells):
    rows = cells // LANES
    total = planes * rows
    part = rows // 2
    flat = jax.ShapeDtypeStruct((total * width, LANES), jnp.float32)
    out_spec = pl.BlockSpec((part * width, LANES), lambda i: (i, 0))
    outs = pl.pallas_call(
        functools.partial(rotate_kernel, width),
        grid=(total // part,),
        out_shape=[flat, flat],
        in_specs=[
            pl.BlockSpec(memory_space=pltpu.SMEM),
            pl.BlockSpec((2 * width, part, LANES), lambda i: (0, i, 0)),
        ],
        out_specs=[out_spec, out_spec],
        compiler_params=pltpu.CompilerParams(vmem_limit_bytes=32 * 1024 * 1024),
    )(mix, fields.reshape(2 * width, total, LANES))

    def whole(flat):
        apart = flat.reshape(planes, rows, width, LANES).transpose(0, 2, 1, 3)
        return apart.reshape(planes, width, cells).transpose(1, 0, 2)

    return tuple(whole(flat) for flat in outs)


def spread(value, axis, source):
    kept = jnp.where(lax.axis_index(axis) == source, value, 0).astype(value.dtype)
    return lax.psum(kept, axis)


def mixing(block, coefficients, source, target, width):
    part_coeffs = lax.dynamic_slice(coefficients, (source * width, target * width), (width, width))
    return jnp.einsum("bxp,bc->cxp", block, part_coeffs, precision=lax.Precision.HIGHEST)


def body(orbitals, potential, coefficients, owners, *, bands, domains):
    width = orbitals.shape[0]
    mine = lax.axis_index("band")
    sources = owners // width
    offsets = owners % width
    layers = domains // width

    def part(source):
        return lax.dynamic_slice(coefficients, (source * width, mine * width), (width, width))

    if bands == 2:
        kept, theirs = part(mine), jnp.zeros((width, width), jnp.float32)
        for turn in range(owners.shape[0]):
            rolled = jnp.roll(part(sources[turn]), offsets[turn], axis=0)
            kept = kept + jnp.where(sources[turn] == mine, rolled, 0.0)
            theirs = theirs + jnp.where(sources[turn] == mine, 0.0, rolled)
        mix = jnp.concatenate([kept, theirs], axis=0)
        fields = run_filter(orbitals, potential, layers, bands)
        return run_rotation(fields, mix, width, *orbitals.shape[1:])
    filtered = run_filter(orbitals, potential, layers, bands).reshape(orbitals.shape)
    rotated = mixing(filtered, coefficients, mine, mine, width)
    for turn in range(owners.shape[0]):
        arrived = spread(filtered, "band", sources[turn])
        rolled = jnp.roll(arrived, -offsets[turn], axis=0)
        rotated = rotated + mixing(rolled, coefficients, sources[turn], mine, width)
    return filtered, rotated


def solution(mesh):
    in_specs = (P("band", "domain", None), P("domain", None), P(), P())
    out_specs = (P("band", "domain", None), P("band", "domain", None))
    step = functools.partial(body, bands=mesh.shape["band"], domains=mesh.shape["domain"])
    return jax.shard_map(step, mesh=mesh, in_specs=in_specs, out_specs=out_specs, check_vma=False)
```

```python
import functools

import jax
import jax.numpy as jnp
from jax import lax
from jax.experimental import pallas as pl
from jax.experimental.pallas import tpu as pltpu
from jax.sharding import PartitionSpec as P

LANES = 128
HALO = 4
PAD = 8
MESH = pl.DeviceIdType.MESH

lap_coeffs = (-205.0 / 72.0, 8.0 / 5.0, -1.0 / 5.0, 8.0 / 315.0, -1.0 / 560.0)
CENTER = 6.0
HALF = 5.0


def stencil_planes(out_store, v, prev, pot, rows, stride, first, count):
    weights = [-0.5 * c / HALF for c in lap_coeffs]
    blocks = rows // 24
    lane = lax.broadcasted_iota(jnp.int32, (8, LANES), 1)
    high = lane >= 64
    zero = jnp.zeros((8, LANES), jnp.float32)

    def block(plane, row):
        base = PAD + (plane + HALO) * stride + row
        here = plane * rows + row

        def at(ref, start):
            return ref[pl.ds(start, 8, stride=3), :]

        near = {t: at(v, base + t) for t in range(-6, 9)}
        for t in range(3):
            x = near[t]
            nxt = near[t + 1] if t < 2 else zero
            prv = near[t - 1] if t > 0 else zero
            total = at(pot, here + t) * x
            odd = None
            for k in range(1, 5):
                up, down = lane < k, lane >= LANES - k
                if t == 1:
                    fill_up = jnp.where(high, 0.0, nxt)
                    fill_down = jnp.where(high, prv, 0.0)
                    up = up | (high & (lane < 64 + k))
                    down = down | ((lane >= 64 - k) & (lane < 64))
                else:
                    fill_up, fill_down = nxt, prv
                plus = pltpu.roll(jnp.where(up, fill_up, x), LANES - k, 1)
                minus = pltpu.roll(jnp.where(down, fill_down, x), k, 1)
                pairs = plus + minus
                pairs = pairs + (at(v, base + t + k * stride) + at(v, base + t - k * stride))
                if k % 2 == 0:
                    jump = 3 * k // 2
                    pairs = pairs + (near[t + jump] + near[t - jump])
                else:
                    low_jump = (3 * k) // 2
                    half = jnp.where(
                        high,
                        near[t + low_jump] + near[t - low_jump - 1],
                        near[t + low_jump + 1] + near[t - low_jump],
                    )
                    half = weights[k] * half
                    odd = half if odd is None else odd + half
                total = total + weights[k] * pairs
            total = total + pltpu.roll(odd, 64, 1)
            if prev is not None:
                total = (total + total) - at(prev, base + t)
            out_store(plane, row + t, total)

    def one_plane(index, carry):
        for number in range(blocks):
            block(first + index, number * 24)
        return carry

    lax.fori_loop(0, count, one_plane, 0)


def filter_kernel(
    layers, bands, planes, rows, stride, orbitals, potential, recv, *refs
):
    group = 4
    own = group * planes
    (v0, v1, v2, v3, pot, go_sem, loaded, packed, pot_stage, local_sem, in_send, in_recv,
     pot_send, pot_recv, halo_send, halo_recv, out_send, out_recv) = refs
    me = lax.axis_index("domain")
    band = lax.axis_index("band")
    g = lax.rem(me, group)
    layer = me // group
    root = layer * group
    left = lax.rem(layer + layers - 1, layers) * group + g
    right = lax.rem(layer + 1, layers) * group + g
    core = root + (g + 1 - 2 * lax.rem(g, 2))
    g_core = g + 1 - 2 * lax.rem(g, 2)
    g_across = lax.rem(g + 2, group)
    g_diag = lax.rem(g_core + 2, group)
    across = root + g_across
    outer = (g == 0) | (g == group - 1)
    inner = (g == 1) | (g == 2)

    load = pltpu.make_async_copy(orbitals, loaded, local_sem.at[0])
    load.start()
    mine_pot = pltpu.make_async_copy(potential, pot_stage.at[g], local_sem.at[1])
    mine_pot.start()

    gap = jnp.zeros((PAD, LANES), jnp.float32)

    def clear(index, carry):
        at = pl.multiple_of((index + HALO) * stride, 8)
        for ref in (v0, v1, v2):
            ref[pl.ds(at, PAD), :] = gap
        return carry

    lax.fori_loop(0, own + 1, clear, 0)
    for index in range(own):
        packed[pl.ds(index * stride + rows, PAD), :] = gap

    barrier = pltpu.get_barrier_semaphore()
    friends = [(root + lax.rem(g + d, group), band) for d in range(1, group)] + [(left, band), (right, band)]
    if bands == 2:
        friends += [(root + d, 1 - band) for d in range(group)]
    for friend in friends:
        pl.semaphore_signal(barrier, inc=1, device_id=friend, device_id_type=MESH)
    load.wait()

    def pack(index, carry):
        for plane in range(planes):
            for q in range(group):
                value = loaded[pl.ds((plane * rows + index * 8) * group + q, 8, stride=group), :]
                at = pl.multiple_of((q * planes + plane) * stride + index * 8, 8)
                packed[pl.ds(at, 8), :] = value
        return carry

    lax.fori_loop(0, rows // 8, pack, 0)
    pl.semaphore_wait(barrier, len(friends))
    share = planes * stride - PAD

    def home_slot(q):
        return v0.at[pl.ds(pl.multiple_of(PAD + (HALO + q * planes) * stride, 8), share), :]

    def orbital_source(q):
        return packed.at[pl.ds(pl.multiple_of(q * planes * stride, 8), share), :]

    def orbital_send(partner):
        q = (g, g_core, g_across, g_diag)[partner]
        return pltpu.make_async_remote_copy(
            orbital_source(q), home_slot(g), in_send.at[partner], in_recv.at[partner],
            device_id=(root + q, band), device_id_type=MESH)

    def orbital_arrival(partner, slot):
        where = home_slot(slot)
        pltpu.make_async_copy(where, where, in_recv.at[partner]).wait()

    length = HALO * stride - PAD
    spots = (PAD, PAD + HALO * stride, PAD + own * stride, PAD + (own + HALO) * stride)

    def halo_copies(level):
        ref = (v0, v1, v2)[level]
        low, first, last, high = (ref.at[pl.ds(s, length), :] for s in spots)
        return (
            pltpu.make_async_remote_copy(
                first, high, halo_send.at[level, 0], halo_recv.at[level, 0],
                device_id=(left, band), device_id_type=MESH),
            pltpu.make_async_remote_copy(
                last, low, halo_send.at[level, 1], halo_recv.at[level, 1],
                device_id=(right, band), device_id_type=MESH),
        )

    pot_core = pltpu.make_async_remote_copy(
        potential, pot_stage.at[g], pot_send.at[1], pot_recv.at[1], device_id=(core, band), device_id_type=MESH)
    parts = 2 if bands == 2 else 1
    cells = potential.shape[1] // parts

    def pot_part(ref, index):
        return ref.at[:, pl.ds(pl.multiple_of(index * cells, LANES), cells)]

    my_part = band if parts == 2 else 0
    arrived = pot_stage.at[g_across]
    pot_across = pltpu.make_async_remote_copy(
        pot_part(potential, my_part), pot_part(pot_stage.at[g], my_part),
        pot_send.at[2], pot_recv.at[2], device_id=(across, band), device_id_type=MESH)
    pot_relay = pltpu.make_async_remote_copy(
        pot_part(arrived, my_part), pot_part(arrived, my_part), pot_send.at[3], pot_recv.at[3],
        device_id=(core, band), device_id_type=MESH)
    if parts == 2:
        other_part = 1 - band
        pot_swap = pltpu.make_async_remote_copy(
            pot_part(arrived, my_part), pot_part(arrived, my_part), pot_send.at[4], pot_recv.at[4],
            device_id=(me, 1 - band), device_id_type=MESH)
        pot_relay_other = pltpu.make_async_remote_copy(
            pot_part(arrived, other_part), pot_part(arrived, other_part), pot_send.at[5], pot_recv.at[5],
            device_id=(core, band), device_id_type=MESH)

    def pass_on():
        pot_across.wait_recv()
        if parts == 2:
            pot_swap.start()
        pot_relay.start()
        if parts == 2:
            pot_swap.wait_recv()
            pot_relay_other.start()

    def take_relayed():
        pot_relay.wait_recv()
        if parts == 2:
            pot_relay_other.wait_recv()

    orbital_send(1).start()
    mine_orbital = pltpu.make_async_copy(orbital_source(g), home_slot(g), in_recv.at[0])
    mine_orbital.start()

    @pl.when(outer)
    def _():
        orbital_send(2).start()
        orbital_send(3).start()

    pot_core.start()
    lower = g < 2

    @pl.when(lower)
    def _():
        orbital_arrival(g, 0)
        halo_copies(0)[0].start()

    @pl.when(jnp.logical_not(lower))
    def _():
        orbital_arrival(group - 1 - g, group - 1)
        halo_copies(0)[1].start()

    @pl.when(outer)
    def _():
        orbital_send(2).wait_send()
        orbital_send(3).wait_send()
        pl.semaphore_signal(go_sem, inc=1, device_id=(core, band), device_id_type=MESH)
        pot_across.start()

    @pl.when(inner)
    def _():
        pl.semaphore_wait(go_sem, 1)
        orbital_send(2).start()
        orbital_send(3).start()

    @pl.when(lower)
    def _():
        orbital_arrival(group - 1 - g, group - 1)
        halo_copies(0)[1].start()

    @pl.when(jnp.logical_not(lower))
    def _():
        orbital_arrival(g, 0)
        halo_copies(0)[0].start()

    @pl.when(inner)
    def _():
        orbital_send(2).wait_send()
        orbital_send(3).wait_send()
        pot_across.start()

    def spread_planes(source, slot, store):
        def step(tile, carry):
            columns = pl.ds(pl.multiple_of(tile * LANES, LANES), LANES)
            store(tile, source[slot, :, columns])
            return carry

        lax.fori_loop(0, rows, step, 0, unroll=8)

    def unpack_pot(slot):
        def store(tile, value):
            scaled = (value - (CENTER + 1.5 * lap_coeffs[0])) * (1.0 / HALF)
            pot[pl.ds(slot * planes * rows + tile, planes, stride=rows), :] = scaled

        spread_planes(pot_stage, slot, store)

    def pot_arrival(partner, slot):
        where = pot_stage.at[slot]
        pltpu.make_async_copy(where, where, pot_recv.at[partner]).wait()
        unpack_pot(slot)

    mine_pot.wait()
    unpack_pot(g)
    pot_arrival(1, g_core)

    @pl.when(inner)
    def _():
        pass_on()

    @pl.when(outer)
    def _():
        take_relayed()

    unpack_pot(jnp.where(inner, g_across, g_diag))

    orbital_arrival(g_core, 1)
    orbital_arrival(lax.rem(g + 2, group), 2)

    def padded(ref):
        def store(plane, row, value):
            ref[pl.ds(PAD + (plane + HALO) * stride + row, 8, stride=3), :] = value
        return store

    def plain(plane, row, value):
        v3[pl.ds(plane * rows + row, 8, stride=3), :] = value

    def level(number, first, count):
        if number == 1:
            stencil_planes(padded(v1), v0, None, pot, rows, stride, first, count)
        elif number == 2:
            stencil_planes(padded(v2), v1, v0, pot, rows, stride, first, count)
        else:
            stencil_planes(plain, v2, v1, pot, rows, stride, first, count)

    share_rows = planes * rows

    def piece_span(home, piece):
        start = 2 * (home % 2) if piece == 0 else 4 * (1 - home % 2)
        return start * rows, (4 if piece == 0 else 2) * rows

    def out_copies(home, piece):
        start, size = piece_span(home, piece)
        source = v3.at[pl.ds(home * planes * rows + start, size), :]
        remote = pltpu.make_async_remote_copy(
            source, recv.at[pl.ds(pl.multiple_of(g * share_rows + start, 8), size), :], out_send.at[0, home, piece], out_recv.at[0, g, piece],
            device_id=(root + home, band), device_id_type=MESH)
        local = pltpu.make_async_copy(
            source, recv.at[pl.ds(pl.multiple_of(g * share_rows + start, 8), size), :], out_recv.at[0, g, piece])
        peer = None
        if bands == 2:
            peer = pltpu.make_async_remote_copy(
                source, recv.at[pl.ds(pl.multiple_of((group + g) * share_rows + start, 8), size), :], out_send.at[1, home, piece],
                out_recv.at[1, g, piece], device_id=(root + home, 1 - band), device_id_type=MESH)
        return remote, local, peer

    def start_out(home, piece):
        remote, local, peer = out_copies(home, piece)
        if peer is not None:
            peer.start()

        @pl.when(g != home)
        def _():
            remote.start()

        @pl.when(g == home)
        def _():
            local.start()

    def edges(number):
        halo_copies(number - 1)[1].wait_recv()
        level(number, 0, 4)
        halo_copies(number)[0].start()
        halo_copies(number - 1)[0].wait_recv()
        level(number, own - 4, 4)
        halo_copies(number)[1].start()

    edges(1)

    @pl.when(inner)
    def _():
        take_relayed()

    @pl.when(outer)
    def _():
        pass_on()

    unpack_pot(jnp.where(inner, g_diag, g_across))
    level(1, 4, own - 8)
    level(2, 4, own - 12)
    level(3, 8, 4)
    start_out(1, 0)
    level(2, own - 8, 4)
    level(3, 12, own - 20)
    start_out(2, 0)
    edges(2)
    level(3, 4, 4)
    start_out(0, 1)
    start_out(1, 1)
    level(3, own - 8, 4)
    start_out(2, 1)
    start_out(3, 1)
    halo_copies(2)[1].wait_recv()
    level(3, 0, 4)
    start_out(0, 0)
    halo_copies(2)[0].wait_recv()
    level(3, own - 4, 4)
    start_out(3, 0)

    mine_start4 = 2 * lax.rem(g, 2) * rows
    mine_start2 = 4 * (1 - lax.rem(g, 2)) * rows
    for peer in range(bands if bands == 2 else 1):
        for q in range(group):
            for piece, start, size in ((0, mine_start4, 4 * rows), (1, mine_start2, 2 * rows)):
                where = recv.at[pl.ds(pl.multiple_of((peer * group + q) * share_rows + start, 8), size), :]
                pltpu.make_async_copy(where, where, out_recv.at[peer, q, piece]).wait()

    orbital_send(1).wait_send()
    for copy in (pot_core, pot_across, pot_relay) + ((pot_swap, pot_relay_other) if parts == 2 else ()):
        copy.wait_send()
    for number in range(3):
        for copy in halo_copies(number):
            copy.wait_send()
    for home in range(group):
        for piece in range(2):
            remote, local, peer = out_copies(home, piece)
            if peer is not None:
                peer.wait_send()

            @pl.when(g != home)
            def _():
                remote.wait_send()


def run_filter(orbitals, potential, layers, bands):
    width, planes, cells = orbitals.shape
    rows = cells // LANES
    stride = rows + PAD
    own = width * planes
    padded_rows = (own + 2 * HALO) * stride + PAD
    f32 = jnp.float32
    count = 2 if bands == 2 else 1
    dma = pltpu.SemaphoreType.DMA
    shape = jax.ShapeDtypeStruct((count * own * rows, LANES), f32)
    any_spec = pl.BlockSpec(memory_space=pl.ANY)
    interleaved = orbitals.transpose(1, 0, 2).reshape(planes, width, rows, LANES)
    interleaved = interleaved.transpose(0, 2, 1, 3).reshape(own * rows, LANES)
    return pl.pallas_call(
        functools.partial(filter_kernel, layers, bands, planes, rows, stride),
        out_shape=shape,
        in_specs=[any_spec, any_spec],
        out_specs=any_spec,
        scratch_shapes=[
            pltpu.VMEM((padded_rows, LANES), f32),
            pltpu.VMEM((padded_rows, LANES), f32),
            pltpu.VMEM((padded_rows, LANES), f32),
            pltpu.VMEM((own * rows, LANES), f32),
            pltpu.VMEM((own * rows, LANES), f32),
            pltpu.SemaphoreType.REGULAR,
            pltpu.VMEM((own * rows, LANES), f32),
            pltpu.VMEM((own * stride, LANES), f32),
            pltpu.VMEM((width, planes, cells), f32),
            dma((2,)), dma((4,)), dma((4,)), dma((6,)), dma((6,)),
            dma((3, 2)), dma((3, 2)), dma((2, 4, 2)), dma((2, 4, 2)),
        ],
        compiler_params=pltpu.CompilerParams(
            collective_id=0, has_side_effects=True, vmem_limit_bytes=60 * 1024 * 1024
        ),
    )(interleaved, potential)


def rotate_kernel(width, mix, fields, out_f, out_r):
    def group_rows(index, carry):
        at = pl.multiple_of(index * 8, 8)
        inputs = [fields[i, pl.ds(at, 8), :] for i in range(2 * width)]
        for c in range(width):
            out_f[pl.ds(at * width + c, 8, stride=width), :] = inputs[c]
            total = mix[0, c] * inputs[0]
            for i in range(1, 2 * width):
                total = total + mix[i, c] * inputs[i]
            out_r[pl.ds(at * width + c, 8, stride=width), :] = total
        return carry

    lax.fori_loop(0, fields.shape[1] // 8, group_rows, 0, unroll=6)


def run_rotation(fields, mix, width, planes, cells):
    rows = cells // LANES
    total = planes * rows
    part = rows // 2
    flat = jax.ShapeDtypeStruct((total * width, LANES), jnp.float32)
    out_spec = pl.BlockSpec((part * width, LANES), lambda i: (i, 0))
    outs = pl.pallas_call(
        functools.partial(rotate_kernel, width),
        grid=(total // part,),
        out_shape=[flat, flat],
        in_specs=[
            pl.BlockSpec(memory_space=pltpu.SMEM),
            pl.BlockSpec((2 * width, part, LANES), lambda i: (0, i, 0)),
        ],
        out_specs=[out_spec, out_spec],
        compiler_params=pltpu.CompilerParams(vmem_limit_bytes=60 * 1024 * 1024),
    )(mix, fields.reshape(2 * width, total, LANES))

    def whole(flat):
        apart = flat.reshape(planes, rows, width, LANES).transpose(0, 2, 1, 3)
        return apart.reshape(planes, width, cells).transpose(1, 0, 2)

    return tuple(whole(flat) for flat in outs)


def spread(value, axis, source):
    kept = jnp.where(lax.axis_index(axis) == source, value, 0).astype(value.dtype)
    return lax.psum(kept, axis)


def mixing(block, coefficients, source, target, width):
    part_coeffs = lax.dynamic_slice(coefficients, (source * width, target * width), (width, width))
    return jnp.einsum("bxp,bc->cxp", block, part_coeffs, precision=lax.Precision.HIGHEST)


def body(orbitals, potential, coefficients, owners, *, bands, domains):
    width = orbitals.shape[0]
    mine = lax.axis_index("band")
    sources = owners // width
    offsets = owners % width
    layers = domains // width

    def part(source):
        return lax.dynamic_slice(coefficients, (source * width, mine * width), (width, width))

    if bands == 2:
        kept, theirs = part(mine), jnp.zeros((width, width), jnp.float32)
        for turn in range(owners.shape[0]):
            rolled = jnp.roll(part(sources[turn]), offsets[turn], axis=0)
            kept = kept + jnp.where(sources[turn] == mine, rolled, 0.0)
            theirs = theirs + jnp.where(sources[turn] == mine, 0.0, rolled)
        mix = jnp.concatenate([kept, theirs], axis=0)
        fields = run_filter(orbitals, potential, layers, bands)
        return run_rotation(fields, mix, width, *orbitals.shape[1:])
    filtered = run_filter(orbitals, potential, layers, bands).reshape(orbitals.shape)
    rotated = mixing(filtered, coefficients, mine, mine, width)
    for turn in range(owners.shape[0]):
        arrived = spread(filtered, "band", sources[turn])
        rolled = jnp.roll(arrived, -offsets[turn], axis=0)
        rotated = rotated + mixing(rolled, coefficients, sources[turn], mine, width)
    return filtered, rotated


def solution(mesh):
    in_specs = (P("band", "domain", None), P("domain", None), P(), P())
    out_specs = (P("band", "domain", None), P("band", "domain", None))
    step = functools.partial(body, bands=mesh.shape["band"], domains=mesh.shape["domain"])
    return jax.shard_map(step, mesh=mesh, in_specs=in_specs, out_specs=out_specs, check_vma=False)
```
